32 devices in a mesh: slab: 2 (over y), brick: 16 (over z, x, core).
Axes of the slice: x: 2, y: 2, z: 4, core: 2. Of those that a mesh axis runs over, the one named last changes fastest.
Arguments:
- inputs: bfloat16 [64, 8, 32, 128], P('brick', None, 'slab'), may hold values from -6 to 6
- pre_first: bfloat16 [64, 8, 32, 128], P('brick', None, 'slab'), may hold values from -8 to 8
- occupancy: int32 [64, 8, 32], P('brick', None, 'slab'), may hold values 0 or 1
- grad_out: bfloat16 [64, 8, 32, 128], P('brick', None, 'slab'), may hold values from -6 to 6
- w_first: bfloat16 [27, 128, 128], replicated, may hold values from -0.109375 to 0.109375
- w_second: bfloat16 [27, 128, 128], replicated, may hold values from -0.109375 to 0.109375
Outputs:
- grad_in: bfloat16 [64, 8, 32, 128], P('brick', None, 'slab')
- grad_first: bfloat16 [27, 128, 128], replicated
- grad_second: bfloat16 [27, 128, 128], replicated
The draws below stay inside these ranges and needn't reach their ends.
All inputs are finite; a program needn't handle non-finite values. No bound on the sum of `occupancy` on one device may be relied on, other than what follows from the above.
Results may differ from the reference program's by a relative error of at most 0.0053.
Values may be sent and summed in bfloat16 or wider, within the bound.
No kernel may reach another device: no remote copies, remote signals or barrier semaphores. Data moves between devices by JAX's collectives and lax.ppermute only.
A program may use at most 64 MiB of HBM per device.

```python
import jax
import jax.numpy as jnp

C = 128
NY = 8
NX = 64
NZ = 32
CELLS = 16384


def with_ends(entries, key, smallest, top_value):
    index_at = [jax.random.randint(jax.random.fold_in(key, axis), (), 0, length) for axis, length in enumerate(entries.shape)]
    widest = entries.shape.index(max(entries.shape))
    next_to = index_at[:widest] + [(index_at[widest] + 1) % entries.shape[widest]] + index_at[widest + 1:]
    return entries.at[tuple(index_at)].set(smallest).at[tuple(next_to)].set(top_value)


def shard_levels(rng, dims, split, least, high):
    def one(position, blocks):
        heights = jax.random.uniform(jax.random.fold_in(jax.random.fold_in(rng, 6), position), (blocks,), jnp.float32, least / len(split), high / len(split))
        return jnp.repeat(jnp.exp(heights), dims[position] // blocks).reshape((-1,) + (1,) * (len(dims) - position - 1))

    gain = one(*split[0])
    for cut in split[1:]:
        gain = gain * one(*cut)
    return gain


def normal_values(own_key, extent, scale, limit, split=(), held_as=jnp.bfloat16):
    array = jax.random.normal(own_key, extent, jnp.float32) * scale
    if len(split) > 0:
        array = shard_levels(own_key, extent, split, -0.22, 0.18) * array
    return jnp.clip(array, min=-limit, max=limit).astype(held_as)


def setup_inputs(seed: int = 0) -> dict:
    arg_keys = jax.random.split(jax.random.key(seed), 7)
    inputs = normal_values(arg_keys[0], (NX, NY, NZ, C), 1.0, 6.0, ((0, 16), (2, 2)))
    pre_first = normal_values(arg_keys[1], (NX, NY, NZ, C), 1.5, 8.0, ((0, 16), (2, 2)))
    occupancy = with_ends((jax.random.randint(arg_keys[2], (NX, NY, NZ), 0, 10) < 1).astype(jnp.int32), jax.random.fold_in(arg_keys[2], 1), 0, 1)
    grad_out = normal_values(arg_keys[3], (NX, NY, NZ, C), 1.0, 6.0, ((0, 16), (2, 2)))
    w_first = normal_values(arg_keys[4], (27, C, C), (27 * C) ** -0.5, 0.109375)
    w_second = normal_values(arg_keys[5], (27, C, C), (27 * C) ** -0.5, 0.109375)
    return dict(inputs=inputs, pre_first=pre_first, occupancy=occupancy, grad_out=grad_out, w_first=w_first, w_second=w_second)


def offsets():
    return [(a, b, c) for a in (-1, 0, 1) for b in (-1, 0, 1) for c in (-1, 0, 1)]

def transpose_conv(field, kernel):
    chans = field.shape[-1]
    total = jnp.zeros((field.shape[0] * field.shape[1] * field.shape[2], chans), jnp.float32)
    for index, (a, b, c) in enumerate(offsets()):
        rolled = jnp.roll(field, shift=(a, b, c), axis=(0, 1, 2)).reshape(-1, chans)
        total = total + jnp.dot(rolled, kernel[index].T, preferred_element_type=jnp.float32)
    return total.reshape(field.shape)

def kernel_grad(left, field):
    chans = field.shape[-1]
    flat_left = left.reshape(-1, chans)
    parts = []
    for a, b, c in offsets():
        rolled = jnp.roll(field, shift=(a, b, c), axis=(0, 1, 2)).reshape(-1, chans)
        parts.append(jnp.dot(flat_left.T, rolled, preferred_element_type=jnp.float32))
    return jnp.stack(parts, axis=0)

def reference(inputs, pre_first, occupancy, grad_out, w_first, w_second):
    scale = 10.0 / jnp.sqrt(jnp.float32(CELLS))
    occ = occupancy.astype(jnp.float32)[..., None]
    pre = pre_first.astype(jnp.float32)
    sig = jax.nn.sigmoid(pre)
    act = (pre * sig * occ).astype(jnp.bfloat16)
    grad_second_pre = (grad_out.astype(jnp.float32) * occ).astype(jnp.bfloat16)
    grad_act = transpose_conv(grad_second_pre, w_second)
    grad_second = (kernel_grad(act, grad_second_pre) * scale).astype(jnp.bfloat16)
    grad_first_pre = (grad_act * occ * sig * (1.0 + pre * (1.0 - sig))).astype(jnp.bfloat16)
    grad_in = (grad_out.astype(jnp.float32) + transpose_conv(grad_first_pre, w_first)).astype(jnp.bfloat16)
    grad_first = (kernel_grad(inputs, grad_first_pre) * scale).astype(jnp.bfloat16)
    return (grad_in, grad_first, grad_second)
```

```python
import functools

import jax
import jax.numpy as jnp
from jax import lax
from jax.experimental import pallas as pl
from jax.experimental.pallas import tpu as pltpu
from jax.sharding import PartitionSpec as P

AXES = ("slab", "brick")
F32 = jnp.float32
BF16 = jnp.bfloat16
OFFSETS = [(a, b, c) for a in (-1, 0, 1) for b in (-1, 0, 1) for c in (-1, 0, 1)]
EMPTY = -9984.0
VMEM_BYTES = 48 * 1024 * 1024


def send(value, slab_from, brick_from):
    slabs, bricks = lax.axis_size("slab"), lax.axis_size("brick")
    pairs = [
        (slab_from(s) * bricks + brick_from(b), s * bricks + b)
        for s in range(slabs)
        for b in range(bricks)
    ]
    return lax.ppermute(value, AXES, pairs)


def same(index):
    return index


def over_slabs(value, brick_from=same):
    slabs = lax.axis_size("slab")
    pieces = []
    for r in range(slabs):
        if r == 0 and brick_from is same:
            pieces.append(value)
        else:
            pieces.append(send(value, lambda s, r=r: (s + r) % slabs, brick_from))
    return pieces


def partner(value, bit):
    return send(value, same, lambda b: b ^ bit)


def shifted(field_ref, a, b, c, start, planes, nz):
    ny = field_ref.shape[2] - 2
    block = field_ref[c + 1, pl.ds(start - a, planes), pl.ds(1 - b, ny), pl.ds(0, nz), :]
    return block.reshape(planes * ny * nz, block.shape[-1])


def put_planes(field_ref, start, planes):
    n, ny, nz, chans = planes.shape
    flat = planes.reshape(n * ny, nz, chans)
    for c in (-1, 0, 1):
        rolled = flat if c == 0 else pltpu.roll(flat, c % nz, 1)
        rolled = rolled.astype(BF16).reshape(n, ny, nz, chans)
        field_ref[c + 1, pl.ds(start, n), pl.ds(1, ny)] = rolled
        field_ref[c + 1, pl.ds(start, n), pl.ds(0, 1)] = rolled[:, ny - 1 :]
        field_ref[c + 1, pl.ds(start, n), pl.ds(ny + 1, 1)] = rolled[:, :1]


def joined(refs, start, count):
    return jnp.concatenate([r[start : start + count].astype(F32) for r in refs], axis=2)


def fill_second(field_ref, own, other, rim_own, rim_other, me):
    width = own[0].shape[0] // 2
    for i in range(width):
        put_planes(field_ref, 2 + width * me + i, joined(own, i, 1))
        put_planes(field_ref, 2 + width * (1 - me) + i, joined(other, i, 1))
    for i in range(2):
        put_planes(field_ref, (2 + 2 * width) * me + i, joined(rim_own, i, 1))
        put_planes(field_ref, (2 + 2 * width) * (1 - me) + i, joined(rim_other, i, 1))


def sigmoid(v):
    return 1.0 / (1.0 + jnp.exp(-v))


def kernel_terms(left_ref, field_ref, start, planes, nz, scratch_ref, index_ref, per, scale):
    chans = left_ref.shape[-1]
    for j in range(per):
        k = jnp.minimum(index_ref[1] * per + j, 26)
        a, b, c = k // 9 - 1, (k // 3) % 3 - 1, k % 3 - 1
        cols = shifted(field_ref, a, b, c, start, planes, nz)
        term = lax.dot_general(
            left_ref[...], cols, (((0,), (0,)), ((), ())), preferred_element_type=F32
        )
        scratch_ref[pl.ds(j * chans, chans), :] = term * scale


def put_chunks(scratch_ref, keep_ref, sent_ref, me, rows):
    for r in range(2 * keep_ref.shape[0]):
        chunk = scratch_ref[pl.ds(pl.multiple_of((me ^ r) * rows, 8), rows), :]
        if r % 2 == 0:
            keep_ref[r // 2] = chunk
        else:
            sent_ref[r // 2] = chunk.astype(BF16)


def split_refs(refs, counts):
    out, at = [], 0
    for n in counts:
        out.append(list(refs[at : at + n]))
        at += n
    return out + [list(refs[at:])]


def second_kernel(slabs, per, scale, index_ref, *refs):
    own, other, rim_own, rim_other, rest = split_refs(refs, [slabs] * 4)
    keep_ref, sent_ref, field_ref, act_ref, scratch_ref = rest
    me = index_ref[0]
    width, (ny, zs, chans) = own[0].shape[0] // 2, own[0].shape[1:]
    nz = zs * slabs
    fill_second(field_ref, own, other, rim_own, rim_other, me)
    for i in range(width):
        for refs_of, who in ((own, me), (other, 1 - me)):
            pre = joined(refs_of, width + i, 1)
            act = (pre * sigmoid(pre)).astype(BF16).reshape(ny * nz, chans)
            at = pl.multiple_of((who * width + i) * ny * nz, ny * nz)
            act_ref[pl.ds(at, ny * nz), :] = act
    kernel_terms(act_ref, field_ref, 2, 2 * width, nz, scratch_ref, index_ref, per, scale)
    put_chunks(scratch_ref, keep_ref, sent_ref, index_ref[2], keep_ref.shape[1])


def first_kernel(slabs, per, scale, index_ref, *refs):
    own, other, rim_own, rim_other, in_own, in_other, rest = split_refs(refs, [slabs] * 6)
    (grad_out_ref, w_second_ref, w_first_ref, grad_in_ref, keep_ref, sent_ref) = rest[:6]
    field_ref, first_ref, left_ref, scratch_ref = rest[6:]
    me = index_ref[0]
    width, (ny, zs, chans) = own[0].shape[0] // 2, own[0].shape[1:]
    nz = zs * slabs
    fill_second(field_ref, own, other, rim_own, rim_other, me)

    def conv(ref, start, planes, depth, w_ref):
        cols = jnp.concatenate(
            [shifted(ref, a, b, c, start, planes, depth) for a, b, c in OFFSETS], axis=1
        )
        out = jnp.dot(cols, w_ref[...], preferred_element_type=F32)
        return out.reshape(planes, ny, depth, chans)

    def put_first(at, pre):
        grad_act = conv(field_ref, at + 1, pre.shape[0], nz, w_second_ref)
        sig = sigmoid(pre)
        put_planes(first_ref, at, grad_act * (sig * (1.0 + pre * (1.0 - sig))))

    for i in range(0, width, 2):
        put_first(1 + width * me + i, joined(own, width + i, 2))
        put_first(1 + width * (1 - me) + i, joined(other, width + i, 2))
    put_first((1 + 2 * width) * me, joined(rim_own, 2, 1))
    put_first((1 + 2 * width) * (1 - me), joined(rim_other, 2, 1))

    back = conv(first_ref, 1 + width * me, width, zs, w_first_ref)
    grad_in_ref[...] = (grad_out_ref[...].astype(F32) + back).astype(BF16)

    for i in range(width):
        for refs_of, who in ((in_own, me), (in_other, 1 - me)):
            rows = joined(refs_of, i, 1).astype(BF16).reshape(ny * nz, chans)
            at = pl.multiple_of((who * width + i) * ny * nz, ny * nz)
            left_ref[pl.ds(at, ny * nz), :] = rows
    kernel_terms(left_ref, first_ref, 1, 2 * width, nz, scratch_ref, index_ref, per, scale)
    put_chunks(scratch_ref, keep_ref, sent_ref, index_ref[2], keep_ref.shape[1])


def vmem(shape, dtype):
    return pltpu.VMEM(shape, dtype)


def call(body, index, operands, out_shape, scratch, flops, name):
    return pl.pallas_call(
        body,
        out_shape=out_shape,
        in_specs=[pl.BlockSpec(memory_space=pltpu.SMEM)]
        + [pl.BlockSpec(memory_space=pltpu.VMEM)] * len(operands),
        out_specs=[pl.BlockSpec(memory_space=pltpu.VMEM)] * len(out_shape),
        scratch_shapes=scratch,
        compiler_params=pltpu.CompilerParams(vmem_limit_bytes=VMEM_BYTES),
        cost_estimate=pl.CostEstimate(flops=flops, bytes_accessed=4 << 20, transcendentals=0),
        name=name,
    )(index, *operands)


def reduce_pairs(keep, sent, pairs):
    held = list(range(0, pairs, 2))
    gone = list(range(1, pairs, 2))
    bits = []
    bit = 1
    while bit < pairs:
        bits.append(bit)
        got = partner(sent, 2 * bit).astype(F32)
        total = keep + got
        nxt = 2 * bit
        if nxt < pairs // 2:
            pick = [i for i, r in enumerate(held) if not r & nxt]
            drop = [i for i, r in enumerate(held) if r & nxt]
            keep = total[pick[0] :: pick[1] - pick[0]] if len(pick) > 1 else total[pick[0]][None]
            sent = total[drop[0] :: drop[1] - drop[0]] if len(drop) > 1 else total[drop[0]][None]
            sent = sent.astype(BF16)
            held = [held[i] for i in pick]
            bit = nxt
        else:
            break
    last = pairs // 2
    mine = total.astype(BF16)
    got = partner(mine, 2 * last)
    whole = (mine.astype(F32) + got[::-1].astype(F32)).astype(BF16)
    pieces = [(whole, held)]
    for bit in reversed(bits):
        array = jnp.concatenate([p for p, _ in pieces], axis=0)
        names = [r for _, n in pieces for r in n]
        got = partner(array, 2 * bit)
        pieces = [(array, names), (got, [r ^ bit for r in names])]
    array = jnp.concatenate([p for p, _ in pieces], axis=0)
    return array, [r for _, n in pieces for r in n]


def place_kernel(slabs, names, index_ref, *refs):
    pieces, (out_ref, scratch_ref) = refs[:-2], refs[-2:]
    rows = pieces[0].shape[1]
    pairs = len(names)
    me, pair, slab = index_ref[0], index_ref[2], index_ref[3]
    for n, piece in enumerate(pieces):
        r, core = n // 2, n % 2
        share = lax.rem(slab + r, slabs) * 2 + (me ^ core)
        for i, distance in enumerate(names):
            at = pl.multiple_of((share * pairs + (pair ^ distance)) * rows, 16)
            scratch_ref[pl.ds(at, rows), :] = piece[i]
    out_ref[...] = scratch_ref[pl.ds(0, out_ref.shape[0]), :]


def per_device(inputs, pre_first, occupancy, grad_out, w_first, w_second):
    width, ny, zs, chans = inputs.shape
    slabs, bricks = lax.axis_size("slab"), lax.axis_size("brick")
    pairs, nz = bricks // 2, zs * slabs
    cells_all = width * bricks * ny * nz
    scale = 10.0 / cells_all**0.5
    per = -(-27 // (2 * slabs))
    while per * chans % (16 * pairs):
        per += 1
    rows = per * chans // pairs
    slab, brick = lax.axis_index("slab"), lax.axis_index("brick")
    me = lax.rem(brick, 2)
    index = jnp.stack([me, slab * 2 + me, brick // 2, slab]).astype(jnp.int32)

    occ = occupancy[..., None] != 0
    masked = jnp.where(occ, grad_out, jnp.zeros_like(grad_out))
    pre = jnp.where(occ, pre_first, jnp.full_like(pre_first, EMPTY))
    both = jnp.concatenate([masked, pre], axis=0)
    odd = me == 1
    rim = jnp.concatenate(
        [
            jnp.where(odd, masked[width - 2 :], masked[:2]),
            jnp.where(odd, pre[width - 1 :], pre[:1]),
        ],
        axis=0,
    )

    def swap(b):
        return (b + 1) % bricks if b % 2 else (b - 1) % bricks

    own = over_slabs(both)
    rim_own = over_slabs(rim, swap)
    other = [partner(v, 1) for v in own]
    rim_other = [partner(v, 1) for v in rim_own]
    in_own = over_slabs(inputs)
    in_other = [partner(v, 1) for v in in_own]

    def stacked(kernel):
        return jnp.transpose(kernel, (0, 2, 1)).reshape(27 * chans, chans)

    shares = [
        jax.ShapeDtypeStruct((pairs // 2, rows, chans), F32),
        jax.ShapeDtypeStruct((pairs // 2, rows, chans), BF16),
    ]
    field = vmem((3, 2 * width + 4, ny + 2, nz, chans), BF16)
    group = 2 * width * ny * nz
    terms = vmem((per * chans, chans), F32)
    around = [*own, *other, *rim_own, *rim_other]
    keep, sent = call(
        functools.partial(second_kernel, slabs, per, scale),
        index,
        around,
        shares,
        [field, vmem((group, chans), BF16), terms],
        2 * group * per * chans * chans,
        "second_kernel_gradient",
    )
    grad_in, keep_first, sent_first = call(
        functools.partial(first_kernel, slabs, per, scale),
        index,
        [*around, *in_own, *in_other, grad_out, stacked(w_second), stacked(w_first)],
        [jax.ShapeDtypeStruct(inputs.shape, BF16), *shares],
        [
            field,
            vmem((3, 2 * width + 2, ny + 2, nz, chans), BF16),
            vmem((group, chans), BF16),
            terms,
        ],
        2 * group * (28 + per) * chans * chans,
        "first_kernel_gradient",
    )

    def finish(keep, sent):
        array, names = reduce_pairs(keep, sent, pairs)
        pieces = []
        for v in over_slabs(array):
            pieces += [v, partner(v, 1)]
        (out,) = call(
            functools.partial(place_kernel, slabs, names),
            index,
            pieces,
            [jax.ShapeDtypeStruct((27 * chans, chans), BF16)],
            [vmem((2 * slabs * per * chans, chans), BF16)],
            0,
            "place",
        )
        return out.reshape(27, chans, chans)

    return (grad_in, finish(keep_first, sent_first), finish(keep, sent))


def solution(mesh):
    in_specs = (
        P("brick", None, "slab", None),
        P("brick", None, "slab", None),
        P("brick", None, "slab"),
        P("brick", None, "slab", None),
        P(),
        P(),
    )
    out_specs = (P("brick", None, "slab", None), P(), P())
    return jax.shard_map(
        per_device, mesh=mesh, in_specs=in_specs, out_specs=out_specs, check_vma=False
    )
```

```python
import functools
import math

import jax
import jax.numpy as jnp
from jax import lax
from jax.experimental import pallas as pl
from jax.experimental.pallas import tpu as pltpu
from jax.sharding import PartitionSpec as P

AXES = ("slab", "brick")
F32 = jnp.float32
BF16 = jnp.bfloat16
OFFSETS = [(a, b, c) for a in (-1, 0, 1) for b in (-1, 0, 1) for c in (-1, 0, 1)]
EMPTY = -9984.0


def send(value, slab_from, brick_from):
    slabs, bricks = lax.axis_size("slab"), lax.axis_size("brick")
    pairs = [
        (slab_from(s) * bricks + brick_from(b), s * bricks + b)
        for s in range(slabs)
        for b in range(bricks)
    ]
    return lax.ppermute(value, AXES, pairs)


def same(index):
    return index


def over_slabs(value, brick_from=same):
    slabs = lax.axis_size("slab")
    pieces = []
    for r in range(slabs):
        if r == 0 and brick_from is same:
            pieces.append(value)
        else:
            pieces.append(send(value, lambda s, r=r: (s + r) % slabs, brick_from))
    return pieces


def partner(value, bit):
    return send(value, same, lambda b: b ^ bit)


def shifted(field_ref, a, b, c, start, planes, nz):
    ny = field_ref.shape[2] - 2
    block = field_ref[c + 1, pl.ds(start - a, planes), pl.ds(1 - b, ny), pl.ds(0, nz), :]
    return block.reshape(planes * ny * nz, block.shape[-1])


def put_planes(field_ref, start, planes):
    n, ny, nz, chans = planes.shape
    flat = planes.reshape(n * ny, nz, chans)
    for c in (-1, 0, 1):
        rolled = flat if c == 0 else pltpu.roll(flat, c % nz, 1)
        rolled = rolled.astype(BF16).reshape(n, ny, nz, chans)
        field_ref[c + 1, pl.ds(start, n), pl.ds(1, ny)] = rolled
        field_ref[c + 1, pl.ds(start, n), pl.ds(0, 1)] = rolled[:, ny - 1 :]
        field_ref[c + 1, pl.ds(start, n), pl.ds(ny + 1, 1)] = rolled[:, :1]


def joined(refs, start, count):
    return jnp.concatenate([r[start : start + count].astype(F32) for r in refs], axis=2)


def fill_second(field_ref, own, other, rim_own, rim_other, me):
    width = own[0].shape[0] // 3
    for i in range(width):
        put_planes(field_ref, 2 + width * me + i, joined(own, i, 1))
        put_planes(field_ref, 2 + width * (1 - me) + i, joined(other, i, 1))
    for i in range(2):
        put_planes(field_ref, (2 + 2 * width) * me + i, joined(rim_own, i, 1))
        put_planes(field_ref, (2 + 2 * width) * (1 - me) + i, joined(rim_other, i, 1))


def sigmoid(v):
    return 1.0 / (1.0 + jnp.exp(-v))


def kernel_terms(left_ref, field_ref, start, planes, nz, scratch_ref, index_ref, per, scale):
    chans = left_ref.shape[-1]
    for j in range(per):
        k = jnp.minimum(index_ref[1] * per + j, 26)
        a, b, c = k // 9 - 1, (k // 3) % 3 - 1, k % 3 - 1
        cols = shifted(field_ref, a, b, c, start, planes, nz)
        term = lax.dot_general(
            left_ref[...], cols, (((0,), (0,)), ((), ())), preferred_element_type=F32
        )
        scratch_ref[pl.ds(j * chans, chans), :] = term * scale


def put_chunks(scratch_ref, keep_ref, sent_refs, me, tensor):
    count, rows = keep_ref.shape[0], keep_ref.shape[1] // 2
    for i in range(count):
        for rest, ref in enumerate((keep_ref, *sent_refs)):
            at = pl.multiple_of((me ^ (4 * i + rest)) * rows, 8)
            chunk = scratch_ref[pl.ds(at, rows), :].astype(ref.dtype)
            ref[i, pl.ds(tensor * rows, rows), :] = chunk


def group_kernel(slabs, per, scale, index_ref, *refs):
    own, other = refs[:slabs], refs[slabs : 2 * slabs]
    rim_own, rim_other = (
        [ref.at[pl.ds(3 * r, 3)] for r in range(slabs)] for ref in refs[2 * slabs : 2 * slabs + 2]
    )
    grad_out_ref, w_second_ref, w_first_ref, grad_in_ref, keep_ref, *refs = refs[2 * slabs + 2 :]
    *sent_refs, field_ref, first_ref, left_ref, scratch_ref = refs
    me, pair = index_ref[0], index_ref[2]
    width, (ny, zs, chans) = own[0].shape[0] // 3, own[0].shape[1:]
    nz = zs * slabs
    fill_second(field_ref, own, other, rim_own, rim_other, me)

    def fill_left(plane):
        for i in range(width):
            for refs_of, who in ((own, me), (other, 1 - me)):
                rows = plane(refs_of, i).astype(BF16).reshape(ny * nz, chans)
                at = pl.multiple_of((who * width + i) * ny * nz, ny * nz)
                left_ref[pl.ds(at, ny * nz), :] = rows

    def conv(ref, start, planes, depth, w_ref):
        cols = jnp.concatenate(
            [shifted(ref, a, b, c, start, planes, depth) for a, b, c in OFFSETS], axis=1
        )
        out = jnp.dot(cols, w_ref[...], preferred_element_type=F32)
        return out.reshape(planes, ny, depth, chans)

    def put_first(at, pre):
        grad_act = conv(field_ref, at + 1, pre.shape[0], nz, w_second_ref)
        sig = sigmoid(pre)
        put_planes(first_ref, at, grad_act * (sig * (1.0 + pre * (1.0 - sig))))

    for i in range(0, width, 2):
        put_first(1 + width * me + i, joined(own, width + i, 2))
        put_first(1 + width * (1 - me) + i, joined(other, width + i, 2))
    put_first((1 + 2 * width) * me, joined(rim_own, 2, 1))
    put_first((1 + 2 * width) * (1 - me), joined(rim_other, 2, 1))

    back = conv(first_ref, 1 + width * me, width, zs, w_first_ref)
    grad_in_ref[...] = (grad_out_ref[...].astype(F32) + back).astype(BF16)

    fill_left(lambda refs_of, i: joined(refs_of, 2 * width + i, 1))
    kernel_terms(left_ref, first_ref, 1, 2 * width, nz, scratch_ref, index_ref, per, scale)
    put_chunks(scratch_ref, keep_ref, sent_refs, pair, 0)

    def act(refs_of, i):
        pre = joined(refs_of, width + i, 1)
        return pre * sigmoid(pre)

    fill_left(act)
    kernel_terms(left_ref, field_ref, 2, 2 * width, nz, scratch_ref, index_ref, per, scale)
    put_chunks(scratch_ref, keep_ref, sent_refs, pair, 1)


def vmem(shape, dtype):
    return pltpu.VMEM(shape, dtype)


def vmem_bytes(scratch):
    held = sum(math.prod(v.shape) * v.dtype.itemsize for v in scratch)
    return (12 << 20) + held * 3 // 2


def call(body, index, operands, out_shape, scratch, flops, name):
    def space(shape):
        return pl.BlockSpec(memory_space=pltpu.SMEM if shape.dtype == jnp.int32 else pltpu.VMEM)

    return pl.pallas_call(
        body,
        out_shape=out_shape,
        in_specs=[space(v) for v in (index, *operands)],
        out_specs=[space(v) for v in out_shape],
        scratch_shapes=scratch,
        compiler_params=pltpu.CompilerParams(vmem_limit_bytes=vmem_bytes(scratch)),
        cost_estimate=pl.CostEstimate(flops=flops, bytes_accessed=4 << 20, transcendentals=0),
        name=name,
    )(index, *operands)


def combine(keep, sent, pairs, slabs):
    total = keep + sum(partner(v, 2 * d).astype(F32) for d, v in enumerate(sent, 1))
    held = list(range(0, pairs, 4))
    middle = [1 << i for i in range(2, pairs.bit_length() - 2)]
    for bit in middle:
        keep = jnp.stack([total[i] for i, r in enumerate(held) if not r & bit])
        sent = jnp.stack([total[i] for i, r in enumerate(held) if r & bit])
        total = keep + partner(sent.astype(BF16), 2 * bit).astype(F32)
        held = [r for r in held if not r & bit]
    mine = lax.reduce_precision(total, 8, 7).astype(BF16)
    got = partner(mine, pairs)
    array = (mine.astype(F32) + got[::-1].astype(F32)).astype(BF16)
    for bit in [*middle[::-1], 2]:
        array = jnp.concatenate([array, partner(array, 2 * bit)], axis=0)
        held = held + [r ^ bit for r in held]
    pieces = {(0, 0): array}
    for r in range(slabs):
        for odd in range(2):
            if r or odd:
                pieces[r, odd] = send(
                    array,
                    lambda s, r=r: (s + r) % slabs,
                    lambda b, odd=odd: b ^ (2 * odd),
                )
    return pieces, held


def place_kernel(slabs, pairs, held, index_ref, *refs):
    pieces, outs, scratch_ref, sems = refs[:-4], refs[-4:-2], refs[-2], refs[-1]
    me, pair, slab = index_ref[0], index_ref[2], index_ref[3]
    length = scratch_ref.shape[2]
    rows = length // pairs
    copies = []
    for core in range(2):
        for r in range(slabs):
            share = lax.rem(slab + r, slabs) * 2 + (me ^ core)
            for t, out_ref in enumerate(outs):
                slot = core * slabs + r
                for odd in range(2):
                    for i, d in enumerate(held):
                        at = pl.multiple_of((pair ^ d ^ odd) * rows, 16)
                        piece = pieces[2 * slot + odd]
                        scratch_ref[t, slot, pl.ds(at, rows), :] = piece[i, pl.ds(t * rows, rows), :]
                full, part = divmod(out_ref.shape[0], length)
                cases = [(share < full, length)] + ([(share == full, part)] if part else [])
                start = pl.multiple_of(share * length, 16)
                for case, size in cases:
                    copy = pltpu.make_async_copy(
                        scratch_ref.at[t, slot, pl.ds(0, size)],
                        out_ref.at[pl.ds(start, size)],
                        sems.at[t, slot],
                    )
                    copies.append((case, copy))
                    pl.when(case)(copy.start)
    for case, copy in copies:
        pl.when(case)(copy.wait)


def place(slabs, pairs, held, index, pieces, rows):
    chans = pieces[0].shape[-1]
    length = pieces[0].shape[1] // 2 * pairs
    shape = jax.ShapeDtypeStruct((rows, chans), BF16)
    scratch = [vmem((2, 2 * slabs, length, chans), BF16)]
    return pl.pallas_call(
        functools.partial(place_kernel, slabs, pairs, held),
        out_shape=[shape] * 2,
        in_specs=[pl.BlockSpec(memory_space=pltpu.SMEM)]
        + [pl.BlockSpec(memory_space=pltpu.VMEM)] * len(pieces),
        out_specs=[pl.BlockSpec(memory_space=pl.ANY)] * 2,
        scratch_shapes=[*scratch, pltpu.SemaphoreType.DMA((2, 2 * slabs))],
        compiler_params=pltpu.CompilerParams(vmem_limit_bytes=vmem_bytes(scratch)),
        name="place",
    )(index, *pieces)


def per_device(inputs, pre_first, occupancy, grad_out, w_first, w_second):
    width, ny, zs, chans = inputs.shape
    slabs, bricks = lax.axis_size("slab"), lax.axis_size("brick")
    pairs, nz = bricks // 2, zs * slabs
    cells_all = width * bricks * ny * nz
    scale = 10.0 / cells_all**0.5
    per = -(-27 // (2 * slabs))
    while per * chans % (16 * pairs):
        per += 1
    rows = per * chans // pairs
    slab, brick = lax.axis_index("slab"), lax.axis_index("brick")
    me = lax.rem(brick, 2)
    index = jnp.stack([me, slab * 2 + me, brick // 2, slab]).astype(jnp.int32)

    occ = occupancy[..., None] != 0
    masked = jnp.where(occ, grad_out, jnp.zeros_like(grad_out))
    pre = jnp.where(occ, pre_first, jnp.full_like(pre_first, EMPTY))
    both = jnp.concatenate([masked, pre, inputs], axis=0)
    odd = me == 1
    rim = jnp.concatenate(
        [
            jnp.where(odd, masked[width - 2 :], masked[:2]),
            jnp.where(odd, pre[width - 1 :], pre[:1]),
        ],
        axis=0,
    )

    def swap(b):
        return (b + 1) % bricks if b % 2 else (b - 1) % bricks

    own = over_slabs(both)
    rim_own = jnp.concatenate(over_slabs(rim, swap), axis=0)

    def stacked(kernel):
        return jnp.transpose(kernel, (0, 2, 1)).reshape(27 * chans, chans)

    w_second, w_first, rim_own, own[-1] = lax.optimization_barrier(
        (stacked(w_second), stacked(w_first), rim_own, own[-1])
    )
    other = [partner(v, 1) for v in own]
    rim_other = partner(rim_own, 1)

    shares = [
        jax.ShapeDtypeStruct((pairs // 4, 2 * rows, chans), dtype)
        for dtype in (F32, BF16, BF16, BF16)
    ]
    group = 2 * width * ny * nz
    grad_in, keep, *sent = call(
        functools.partial(group_kernel, slabs, per, scale),
        index,
        [*own, *other, rim_own, rim_other, grad_out, w_second, w_first],
        [jax.ShapeDtypeStruct(inputs.shape, BF16), *shares],
        [
            vmem((3, 2 * width + 4, ny + 2, nz, chans), BF16),
            vmem((3, 2 * width + 2, ny + 2, nz, chans), BF16),
            vmem((group, chans), BF16),
            vmem((per * chans, chans), F32),
        ],
        2 * group * (28 + 2 * per) * chans * chans,
        "group",
    )
    pieces, held = combine(keep, sent, pairs, slabs)
    pieces = [pieces[r, odd] for r in range(slabs) for odd in range(2)]
    pieces += [partner(v, 1) for v in pieces]
    outs = place(slabs, pairs, held, index, pieces, 27 * chans)
    grad_first, grad_second = (out.reshape(27, chans, chans) for out in outs)
    return (grad_in, grad_first, grad_second)


def solution(mesh):
    in_specs = (
        P("brick", None, "slab", None),
        P("brick", None, "slab", None),
        P("brick", None, "slab"),
        P("brick", None, "slab", None),
        P(),
        P(),
    )
    out_specs = (P("brick", None, "slab", None), P(), P())
    return jax.shard_map(
        per_device, mesh=mesh, in_specs=in_specs, out_specs=out_specs, check_vma=False
    )
```

```python
import functools
import math

import jax
import jax.numpy as jnp
from jax import lax
from jax.experimental import pallas as pl
from jax.experimental.pallas import tpu as pltpu
from jax.sharding import PartitionSpec as P

AXES = ("slab", "brick")
F32 = jnp.float32
BF16 = jnp.bfloat16
OFFSETS = [(a, b, c) for a in (-1, 0, 1) for b in (-1, 0, 1) for c in (-1, 0, 1)]
EMPTY = -9984.0


def send(value, slab_from, brick_from):
    slabs, bricks = lax.axis_size("slab"), lax.axis_size("brick")
    pairs = [
        (slab_from(s) * bricks + brick_from(b), s * bricks + b)
        for s in range(slabs)
        for b in range(bricks)
    ]
    return lax.ppermute(value, AXES, pairs)


def same(index):
    return index


def over_slabs(value, brick_from=same):
    slabs = lax.axis_size("slab")
    pieces = []
    for r in range(slabs):
        if r == 0 and brick_from is same:
            pieces.append(value)
        else:
            pieces.append(send(value, lambda s, r=r: (s + r) % slabs, brick_from))
    return pieces


def partner(value, bit):
    return send(value, same, lambda b: b ^ bit)


def shifted(field_ref, a, b, c, start, planes, nz):
    ny = field_ref.shape[2] - 2
    block = field_ref[c + 1, pl.ds(start - a, planes), pl.ds(1 - b, ny), pl.ds(0, nz), :]
    return block.reshape(planes * ny * nz, block.shape[-1])


def put_planes(field_ref, start, planes):
    n, ny, nz, chans = planes.shape
    flat = planes.reshape(n * ny, nz, chans)
    for c in (-1, 0, 1):
        rolled = flat if c == 0 else pltpu.roll(flat, c % nz, 1)
        rolled = rolled.astype(BF16).reshape(n, ny, nz, chans)
        field_ref[c + 1, pl.ds(start, n), pl.ds(1, ny)] = rolled
        field_ref[c + 1, pl.ds(start, n), pl.ds(0, 1)] = rolled[:, ny - 1 :]
        field_ref[c + 1, pl.ds(start, n), pl.ds(ny + 1, 1)] = rolled[:, :1]


def joined(refs, start, count):
    return jnp.concatenate([r[start : start + count].astype(F32) for r in refs], axis=2)


def fill_second(field_ref, own, other, rim_own, rim_other, me):
    width = own[0].shape[0] // 3
    for i in range(width):
        put_planes(field_ref, 2 + width * me + i, joined(own, i, 1))
        put_planes(field_ref, 2 + width * (1 - me) + i, joined(other, i, 1))
    for i in range(2):
        put_planes(field_ref, (2 + 2 * width) * me + i, joined(rim_own, i, 1))
        put_planes(field_ref, (2 + 2 * width) * (1 - me) + i, joined(rim_other, i, 1))


def sigmoid(v):
    return 1.0 / (1.0 + jnp.exp(-v))


def kernel_terms(left_ref, field_ref, start, planes, nz, scratch_ref, index_ref, per, scale):
    chans = left_ref.shape[-1]

    def step(j):
        k = jnp.minimum(index_ref[1] * per + j, 26)
        a, b, c = k // 9 - 1, (k // 3) % 3 - 1, k % 3 - 1
        cols = shifted(field_ref, a, b, c, start, planes, nz)
        term = lax.dot_general(
            left_ref[...], cols, (((0,), (0,)), ((), ())), preferred_element_type=F32
        )
        scratch_ref[pl.ds(pl.multiple_of(j * chans, chans), chans), :] = term * scale

    if left_ref.shape[0] <= 2048:
        for j in range(per):
            step(j)
    else:
        lax.fori_loop(0, per, lambda j, carry: (step(j), carry)[1], 0)


def put_chunks(scratch_ref, keep_ref, sent_refs, me, tensor):
    count, rows = keep_ref.shape[0], keep_ref.shape[1] // 2
    for i in range(count):
        for rest, ref in enumerate((keep_ref, *sent_refs)):
            at = pl.multiple_of((me ^ (4 * i + rest)) * rows, 8)
            chunk = scratch_ref[pl.ds(at, rows), :].astype(ref.dtype)
            ref[i, pl.ds(tensor * rows, rows), :] = chunk


def group_kernel(slabs, per, scale, index_ref, *refs):
    own, other = refs[:slabs], refs[slabs : 2 * slabs]
    rim_own, rim_other = (
        [ref.at[pl.ds(3 * r, 3)] for r in range(slabs)] for ref in refs[2 * slabs : 2 * slabs + 2]
    )
    grad_out_ref, w_second_ref, w_first_ref, grad_in_ref, keep_ref, *refs = refs[2 * slabs + 2 :]
    *sent_refs, field_ref, first_ref, pre_ref, left_ref, parts_ref, wide_ref, scratch_ref = refs
    me, pair = index_ref[0], index_ref[2]
    width, (ny, zs, chans) = own[0].shape[0] // 3, own[0].shape[1:]
    nz = zs * slabs
    unrolled = ny * nz <= 256
    fill_second(field_ref, own, other, rim_own, rim_other, me)

    def products(ref, start, depth, w_ref):
        cols = jnp.concatenate(
            [shifted(ref, 0, b, c, start, 1, depth) for _, b, c in OFFSETS[:9]], axis=1
        )
        return lax.dot_general(
            cols, w_ref[...], (((1,), (1,)), ((), ())), preferred_element_type=F32
        )

    def conv(ref, start, planes, depth, w_ref, put):
        def out(i, part):
            total = sum(part(i - 1 - a)[:, (a + 1) * chans : (a + 2) * chans] for a in (-1, 0, 1))
            put(i - 2, total.reshape(1, ny, depth, chans))

        if unrolled:
            parts = []
            for i in range(planes + 2):
                parts.append(products(ref, start - 1 + i, depth, w_ref))
                if i >= 2:
                    out(i, parts.__getitem__)
            return

        rows = pl.ds(0, ny * depth)

        def step(i, carry):
            parts_ref[i % 3, rows] = products(ref, start - 1 + i, depth, w_ref)
            pl.when(i >= 2)(lambda: out(i, lambda j: parts_ref[(j + 3) % 3, rows]))
            return carry

        lax.fori_loop(0, planes + 2, step, 0)

    def pre_of(i):
        return pre_ref[pl.ds(i, 1)]

    def put_pre(refs_of, i, at):
        pre_ref[pl.ds(at, 1)] = joined(refs_of, i, 1)

    for i in range(width):
        put_pre(own, width + i, 1 + width * me + i)
        put_pre(other, width + i, 1 + width * (1 - me) + i)
    put_pre(rim_own, 2, (1 + 2 * width) * me)
    put_pre(rim_other, 2, (1 + 2 * width) * (1 - me))

    def put_first(i, grad_act):
        pre = pre_of(i)
        sig = sigmoid(pre)
        put_planes(first_ref, i, grad_act * (sig * (1.0 + pre * (1.0 - sig))))

    def put_grad_in(i, back):
        grad_in_ref[pl.ds(i, 1)] = (grad_out_ref[pl.ds(i, 1)].astype(F32) + back).astype(BF16)

    def widened(w_ref):
        for k in range(27):
            a, bc = divmod(k, 9)
            wide_ref[pl.ds(a * chans, chans), pl.ds(bc * chans, chans)] = w_ref[k]
        return wide_ref

    conv(field_ref, 1, 2 * width + 2, nz, widened(w_second_ref), put_first)
    conv(first_ref, 1 + width * me, width, zs, widened(w_first_ref), put_grad_in)

    for i in range(width):
        for refs_of, who in ((own, me), (other, 1 - me)):
            rows = joined(refs_of, 2 * width + i, 1).astype(BF16).reshape(ny * nz, chans)
            at = pl.multiple_of((who * width + i) * ny * nz, ny * nz)
            left_ref[pl.ds(at, ny * nz), :] = rows
    kernel_terms(left_ref, first_ref, 1, 2 * width, nz, scratch_ref, index_ref, per, scale)
    put_chunks(scratch_ref, keep_ref, sent_refs, pair, 0)

    for i in range(2 * width):
        pre = pre_of(1 + i)
        act = (pre * sigmoid(pre)).astype(BF16)
        left_ref[pl.ds(i * ny * nz, ny * nz), :] = act.reshape(ny * nz, chans)
    kernel_terms(left_ref, field_ref, 2, 2 * width, nz, scratch_ref, index_ref, per, scale)
    put_chunks(scratch_ref, keep_ref, sent_refs, pair, 1)


def vmem(shape, dtype):
    return pltpu.VMEM(shape, dtype)


def vmem_bytes(scratch):
    held = sum(math.prod(v.shape) * v.dtype.itemsize for v in scratch)
    return (12 << 20) + held * 3 // 2


def call(body, index, operands, out_shape, scratch, flops, name):
    def space(shape):
        return pl.BlockSpec(memory_space=pltpu.SMEM if shape.dtype == jnp.int32 else pltpu.VMEM)

    return pl.pallas_call(
        body,
        out_shape=out_shape,
        in_specs=[space(v) for v in (index, *operands)],
        out_specs=[space(v) for v in out_shape],
        scratch_shapes=scratch,
        compiler_params=pltpu.CompilerParams(vmem_limit_bytes=vmem_bytes(scratch)),
        cost_estimate=pl.CostEstimate(flops=flops, bytes_accessed=4 << 20, transcendentals=0),
        name=name,
    )(index, *operands)


def combine(keep, sent, pairs, slabs):
    total = keep + sum(partner(v, 2 * d).astype(F32) for d, v in enumerate(sent, 1))
    held = list(range(0, pairs, 4))
    middle = [1 << i for i in range(2, pairs.bit_length() - 2)]
    for bit in middle:
        keep = jnp.stack([total[i] for i, r in enumerate(held) if not r & bit])
        sent = jnp.stack([total[i] for i, r in enumerate(held) if r & bit])
        total = keep + partner(sent.astype(BF16), 2 * bit).astype(F32)
        held = [r for r in held if not r & bit]
    mine = lax.reduce_precision(total, 8, 7).astype(BF16)
    got = partner(mine, pairs)
    array = (mine.astype(F32) + got[::-1].astype(F32)).astype(BF16)
    for bit in [*middle[::-1], 2]:
        array = jnp.concatenate([array, partner(array, 2 * bit)], axis=0)
        held = held + [r ^ bit for r in held]
    pieces = {(0, 0): array}
    for r in range(slabs):
        for odd in range(2):
            if r or odd:
                pieces[r, odd] = send(
                    array,
                    lambda s, r=r: (s + r) % slabs,
                    lambda b, odd=odd: b ^ (2 * odd),
                )
    return pieces, held


def place_kernel(slabs, pairs, held, index_ref, *refs):
    pieces, outs, scratch_ref, sems = refs[:-4], refs[-4:-2], refs[-2], refs[-1]
    me, pair, slab = index_ref[0], index_ref[2], index_ref[3]
    length = scratch_ref.shape[2]
    rows = length // pairs
    copies = []
    for core in range(2):
        for r in range(slabs):
            share = lax.rem(slab + r, slabs) * 2 + (me ^ core)
            for t, out_ref in enumerate(outs):
                slot = core * slabs + r
                for odd in range(2):
                    for i, d in enumerate(held):
                        at = pl.multiple_of((pair ^ d ^ odd) * rows, 16)
                        piece = pieces[2 * slot + odd]
                        scratch_ref[t, slot, pl.ds(at, rows), :] = piece[i, pl.ds(t * rows, rows), :]
                full, part = divmod(out_ref.shape[0], length)
                cases = [(share < full, length)] + ([(share == full, part)] if part else [])
                start = pl.multiple_of(share * length, 16)
                for case, size in cases:
                    copy = pltpu.make_async_copy(
                        scratch_ref.at[t, slot, pl.ds(0, size)],
                        out_ref.at[pl.ds(start, size)],
                        sems.at[t, slot],
                    )
                    copies.append((case, copy))
                    pl.when(case)(copy.start)
    for case, copy in copies:
        pl.when(case)(copy.wait)


def place(slabs, pairs, held, index, pieces, rows):
    chans = pieces[0].shape[-1]
    length = pieces[0].shape[1] // 2 * pairs
    shape = jax.ShapeDtypeStruct((rows, chans), BF16)
    scratch = [vmem((2, 2 * slabs, length, chans), BF16)]
    return pl.pallas_call(
        functools.partial(place_kernel, slabs, pairs, held),
        out_shape=[shape] * 2,
        in_specs=[pl.BlockSpec(memory_space=pltpu.SMEM)]
        + [pl.BlockSpec(memory_space=pltpu.VMEM)] * len(pieces),
        out_specs=[pl.BlockSpec(memory_space=pl.ANY)] * 2,
        scratch_shapes=[*scratch, pltpu.SemaphoreType.DMA((2, 2 * slabs))],
        compiler_params=pltpu.CompilerParams(vmem_limit_bytes=vmem_bytes(scratch)),
        name="place",
    )(index, *pieces)


def per_device(inputs, pre_first, occupancy, grad_out, w_first, w_second):
    width, ny, zs, chans = inputs.shape
    slabs, bricks = lax.axis_size("slab"), lax.axis_size("brick")
    pairs, nz = bricks // 2, zs * slabs
    cells_all = width * bricks * ny * nz
    scale = 10.0 / cells_all**0.5
    per = -(-27 // (2 * slabs))
    while per * chans % (16 * pairs):
        per += 1
    rows = per * chans // pairs
    slab, brick = lax.axis_index("slab"), lax.axis_index("brick")
    me = lax.rem(brick, 2)
    index = jnp.stack([me, slab * 2 + me, brick // 2, slab]).astype(jnp.int32)

    occ = occupancy[..., None] != 0
    masked = jnp.where(occ, grad_out, jnp.zeros_like(grad_out))
    pre = jnp.where(occ, pre_first, jnp.full_like(pre_first, EMPTY))
    both = jnp.concatenate([masked, pre, inputs], axis=0)
    odd = me == 1
    rim = jnp.concatenate(
        [
            jnp.where(odd, masked[width - 2 :], masked[:2]),
            jnp.where(odd, pre[width - 1 :], pre[:1]),
        ],
        axis=0,
    )

    def swap(b):
        return (b + 1) % bricks if b % 2 else (b - 1) % bricks

    own = over_slabs(both)
    rim_own = jnp.concatenate(over_slabs(rim, swap), axis=0)

    rim_own, own[-1] = lax.optimization_barrier((rim_own, own[-1]))
    other = [partner(v, 1) for v in own]
    rim_other = partner(rim_own, 1)

    shares = [
        jax.ShapeDtypeStruct((pairs // 4, 2 * rows, chans), dtype)
        for dtype in (F32, BF16, BF16, BF16)
    ]
    group = 2 * width * ny * nz
    grad_in, keep, *sent = call(
        functools.partial(group_kernel, slabs, per, scale),
        index,
        [*own, *other, rim_own, rim_other, grad_out, w_second, w_first],
        [jax.ShapeDtypeStruct(inputs.shape, BF16), *shares],
        [
            vmem((3, 2 * width + 4, ny + 2, nz, chans), BF16),
            vmem((3, 2 * width + 2, ny + 2, nz, chans), BF16),
            vmem((2 * width + 2, ny, nz, chans), F32),
            vmem((group, chans), BF16),
            vmem((3, ny * nz, 3 * chans), F32),
            vmem((3 * chans, 9 * chans), BF16),
            vmem((per * chans, chans), F32),
        ],
        2 * group * (28 + 2 * per) * chans * chans,
        "group",
    )
    pieces, held = combine(keep, sent, pairs, slabs)
    pieces = [pieces[r, odd] for r in range(slabs) for odd in range(2)]
    pieces += [partner(v, 1) for v in pieces]
    outs = place(slabs, pairs, held, index, pieces, 27 * chans)
    grad_first, grad_second = (out.reshape(27, chans, chans) for out in outs)
    return (grad_in, grad_first, grad_second)


def solution(mesh):
    in_specs = (
        P("brick", None, "slab", None),
        P("brick", None, "slab", None),
        P("brick", None, "slab"),
        P("brick", None, "slab", None),
        P(),
        P(),
    )
    out_specs = (P("brick", None, "slab", None), P(), P())
    return jax.shard_map(
        per_device, mesh=mesh, in_specs=in_specs, out_specs=out_specs, check_vma=False
    )
```

```python
import functools
import math

import jax
import jax.numpy as jnp
from jax import lax
from jax.experimental import pallas as pl
from jax.experimental.pallas import tpu as pltpu
from jax.sharding import PartitionSpec as P

AXES = ("slab", "brick")
F32 = jnp.float32
BF16 = jnp.bfloat16
OFFSETS = [(a, b, c) for a in (-1, 0, 1) for b in (-1, 0, 1) for c in (-1, 0, 1)]
EMPTY = -9984.0


def send(value, slab_from, brick_from):
    slabs, bricks = lax.axis_size("slab"), lax.axis_size("brick")
    pairs = [
        (slab_from(s) * bricks + brick_from(b), s * bricks + b)
        for s in range(slabs)
        for b in range(bricks)
    ]
    return lax.ppermute(value, AXES, pairs)


def same(index):
    return index


def over_slabs(value, brick_from=same):
    slabs = lax.axis_size("slab")
    pieces = []
    for r in range(slabs):
        if r == 0 and brick_from is same:
            pieces.append(value)
        else:
            pieces.append(send(value, lambda s, r=r: (s + r) % slabs, brick_from))
    return pieces


def partner(value, bit):
    return send(value, same, lambda b: b ^ bit)


def shifted(field_ref, a, b, c, start, planes, nz):
    ny = field_ref.shape[2] - 2
    block = field_ref[c + 1, pl.ds(start - a, planes), pl.ds(1 - b, ny), pl.ds(0, nz), :]
    return block.reshape(planes * ny * nz, block.shape[-1])


def put_planes(field_ref, start, planes):
    n, ny, nz, chans = planes.shape
    flat = planes.reshape(n * ny, nz, chans)
    for c in (-1, 0, 1):
        rolled = flat if c == 0 else pltpu.roll(flat, c % nz, 1)
        rolled = rolled.astype(BF16).reshape(n, ny, nz, chans)
        field_ref[c + 1, pl.ds(start, n), pl.ds(1, ny)] = rolled
        field_ref[c + 1, pl.ds(start, n), pl.ds(0, 1)] = rolled[:, ny - 1 :]
        field_ref[c + 1, pl.ds(start, n), pl.ds(ny + 1, 1)] = rolled[:, :1]


def joined(refs, start, count):
    return jnp.concatenate([r[start : start + count].astype(F32) for r in refs], axis=2)


def fill_second(field_ref, own, other, rim_own, rim_other, me):
    width = own[0].shape[0] // 2
    for i in range(width):
        put_planes(field_ref, 2 + width * me + i, joined(own, i, 1))
        put_planes(field_ref, 2 + width * (1 - me) + i, joined(other, i, 1))
    for i in range(2):
        put_planes(field_ref, (2 + 2 * width) * me + i, joined(rim_own, i, 1))
        put_planes(field_ref, (2 + 2 * width) * (1 - me) + i, joined(rim_other, i, 1))


def sigmoid(v):
    return 1.0 / (1.0 + jnp.exp(-v))


def kernel_terms(left_ref, field_ref, start, planes, nz, scratch_ref, index_ref, per, scale):
    chans = left_ref.shape[-1]

    def step(j):
        k = jnp.minimum(index_ref[1] * per + j, 26)
        a, b, c = k // 9 - 1, (k // 3) % 3 - 1, k % 3 - 1
        cols = shifted(field_ref, a, b, c, start, planes, nz)
        term = lax.dot_general(
            left_ref[...], cols, (((0,), (0,)), ((), ())), preferred_element_type=F32
        )
        scratch_ref[pl.ds(pl.multiple_of(j * chans, chans), chans), :] = term * scale

    if left_ref.shape[0] <= 2048:
        for j in range(per):
            step(j)
    else:
        lax.fori_loop(0, per, lambda j, carry: (step(j), carry)[1], 0)


def put_chunks(scratch_ref, keep_ref, sent_refs, me, tensor):
    count, rows = keep_ref.shape[0], keep_ref.shape[1] // 2
    for i in range(count):
        for rest, ref in enumerate((keep_ref, *sent_refs)):
            at = pl.multiple_of((me ^ (4 * i + rest)) * rows, 8)
            chunk = scratch_ref[pl.ds(at, rows), :].astype(ref.dtype)
            ref[i, pl.ds(tensor * rows, rows), :] = chunk


def convolve(ref, start, planes, depth, w_ref, parts_ref, put):
    ny, chans = ref.shape[2] - 2, ref.shape[4]

    def products(at):
        cols = jnp.concatenate(
            [shifted(ref, 0, b, c, at, 1, depth) for _, b, c in OFFSETS[:9]], axis=1
        )
        return jnp.dot(cols, w_ref[...], preferred_element_type=F32)

    def out(i, part):
        total = sum(part(i - 1 - a)[:, (a + 1) * chans : (a + 2) * chans] for a in (-1, 0, 1))
        put(i - 2, total.reshape(1, ny, depth, chans))

    if ny * depth <= 256:
        parts = []
        for i in range(planes + 2):
            parts.append(products(start - 1 + i))
            if i >= 2:
                out(i, parts.__getitem__)
        return

    rows = pl.ds(0, ny * depth)

    def step(i, carry):
        parts_ref[i % 3, rows] = products(start - 1 + i)
        pl.when(i >= 2)(lambda: out(i, lambda j: parts_ref[(j + 3) % 3, rows]))
        return carry

    lax.fori_loop(0, planes + 2, step, 0)


def widen_kernel(*refs):
    half = len(refs) // 2
    for w_ref, wide_ref in zip(refs[1 : half + 1], refs[half + 1 :], strict=True):
        chans = w_ref.shape[1]
        for k in range(27):
            a, bc = divmod(k, 9)
            block = jnp.transpose(w_ref[k].astype(F32)).astype(BF16)
            wide_ref[pl.ds(bc * chans, chans), pl.ds(a * chans, chans)] = block


def grad_in_kernel(index_ref, near_ref, grad_out_ref, w_ref, grad_in_ref, field_ref, parts_ref):
    planes, padded, nz, chans = near_ref.shape
    width, ny, zs, _ = grad_out_ref.shape
    for i in range(planes):
        put_planes(field_ref, i, near_ref[pl.ds(i, 1), pl.ds(1, ny)].astype(F32))

    def put(i, back):
        grad_in_ref[pl.ds(i, 1)] = (grad_out_ref[pl.ds(i, 1)].astype(F32) + back).astype(BF16)

    convolve(field_ref, 1, width, zs, w_ref, parts_ref, put)


def group_kernel(slabs, per, scale, index_ref, *refs):
    own, other, in_own, in_other = (refs[i * slabs : (i + 1) * slabs] for i in range(4))
    refs = refs[2 * slabs :]
    rim_own, rim_other = (
        [ref.at[pl.ds(3 * r, 3)] for r in range(slabs)] for ref in refs[2 * slabs : 2 * slabs + 2]
    )
    w_second_ref, near_ref, keep_ref, *refs = refs[2 * slabs + 2 :]
    *sent_refs, field_ref, first_ref, pre_ref, left_ref, parts_ref, scratch_ref = refs
    me, pair = index_ref[0], index_ref[2]
    width, ny, zs, chans = in_own[0].shape
    nz = zs * slabs
    fill_second(field_ref, own, other, rim_own, rim_other, me)

    def pre_of(i):
        return pre_ref[pl.ds(i, 1)]

    def put_pre(refs_of, i, at):
        pre_ref[pl.ds(at, 1)] = joined(refs_of, i, 1)

    for i in range(width):
        put_pre(own, width + i, 1 + width * me + i)
        put_pre(other, width + i, 1 + width * (1 - me) + i)
    put_pre(rim_own, 2, (1 + 2 * width) * me)
    put_pre(rim_other, 2, (1 + 2 * width) * (1 - me))

    def put_first(i, grad_act):
        pre = pre_of(i)
        sig = sigmoid(pre)
        put_planes(first_ref, i, grad_act * (sig * (1.0 + pre * (1.0 - sig))))

    convolve(field_ref, 1, 2 * width + 2, nz, w_second_ref, parts_ref, put_first)
    near_ref[...] = first_ref[1, pl.ds(width * me, width + 2)]

    for i in range(width):
        for refs_of, who in ((in_own, me), (in_other, 1 - me)):
            rows = joined(refs_of, i, 1).astype(BF16).reshape(ny * nz, chans)
            at = pl.multiple_of((who * width + i) * ny * nz, ny * nz)
            left_ref[pl.ds(at, ny * nz), :] = rows
    kernel_terms(left_ref, first_ref, 1, 2 * width, nz, scratch_ref, index_ref, per, scale)
    put_chunks(scratch_ref, keep_ref, sent_refs, pair, 0)

    for i in range(2 * width):
        pre = pre_of(1 + i)
        act = (pre * sigmoid(pre)).astype(BF16)
        left_ref[pl.ds(i * ny * nz, ny * nz), :] = act.reshape(ny * nz, chans)
    kernel_terms(left_ref, field_ref, 2, 2 * width, nz, scratch_ref, index_ref, per, scale)
    put_chunks(scratch_ref, keep_ref, sent_refs, pair, 1)


def vmem(shape, dtype):
    return pltpu.VMEM(shape, dtype)


def vmem_bytes(scratch):
    held = sum(math.prod(v.shape) * v.dtype.itemsize for v in scratch)
    return (12 << 20) + held * 3 // 2


def call(body, index, operands, out_shape, scratch, flops, name):
    def space(shape):
        return pl.BlockSpec(memory_space=pltpu.SMEM if shape.dtype == jnp.int32 else pltpu.VMEM)

    return pl.pallas_call(
        body,
        out_shape=out_shape,
        in_specs=[space(v) for v in (index, *operands)],
        out_specs=[space(v) for v in out_shape],
        scratch_shapes=scratch,
        compiler_params=pltpu.CompilerParams(vmem_limit_bytes=vmem_bytes(scratch)),
        cost_estimate=pl.CostEstimate(flops=flops, bytes_accessed=4 << 20, transcendentals=0),
        name=name,
    )(index, *operands)


def combine(keep, sent, pairs, slabs, beside):
    total = keep + sum(partner(v, 2 * d).astype(F32) for d, v in enumerate(sent, 1))
    held = list(range(0, pairs, 4))
    middle = [1 << i for i in range(2, pairs.bit_length() - 2)]
    for bit in middle:
        keep = jnp.stack([total[i] for i, r in enumerate(held) if not r & bit])
        sent = jnp.stack([total[i] for i, r in enumerate(held) if r & bit])
        total = keep + partner(sent.astype(BF16), 2 * bit).astype(F32)
        held = [r for r in held if not r & bit]
    mine = lax.reduce_precision(total, 8, 7).astype(BF16)
    got = partner(mine, pairs)
    got, beside = lax.optimization_barrier((got, beside))
    array = (mine.astype(F32) + got[::-1].astype(F32)).astype(BF16)
    for bit in [*middle[::-1], 2]:
        array = jnp.concatenate([array, partner(array, 2 * bit)], axis=0)
        held = held + [r ^ bit for r in held]
    pieces = {(0, 0): array}
    for r in range(slabs):
        for odd in range(2):
            if r or odd:
                pieces[r, odd] = send(
                    array,
                    lambda s, r=r: (s + r) % slabs,
                    lambda b, odd=odd: b ^ (2 * odd),
                )
    return pieces, held, beside


def place_kernel(slabs, pairs, held, index_ref, *refs):
    pieces, outs, scratch_ref, sems = refs[:-4], refs[-4:-2], refs[-2], refs[-1]
    me, pair, slab = index_ref[0], index_ref[2], index_ref[3]
    length = scratch_ref.shape[2]
    rows = length // pairs
    copies = []
    for core in range(2):
        for r in range(slabs):
            share = lax.rem(slab + r, slabs) * 2 + (me ^ core)
            for t, out_ref in enumerate(outs):
                slot = core * slabs + r
                for odd in range(2):
                    for i, d in enumerate(held):
                        at = pl.multiple_of((pair ^ d ^ odd) * rows, 16)
                        piece = pieces[2 * slot + odd]
                        scratch_ref[t, slot, pl.ds(at, rows), :] = piece[i, pl.ds(t * rows, rows), :]
                full, part = divmod(out_ref.shape[0], length)
                cases = [(share < full, length)] + ([(share == full, part)] if part else [])
                start = pl.multiple_of(share * length, 16)
                for case, size in cases:
                    copy = pltpu.make_async_copy(
                        scratch_ref.at[t, slot, pl.ds(0, size)],
                        out_ref.at[pl.ds(start, size)],
                        sems.at[t, slot],
                    )
                    copies.append((case, copy))
                    pl.when(case)(copy.start)
    for case, copy in copies:
        pl.when(case)(copy.wait)


def place(slabs, pairs, held, index, pieces, rows):
    chans = pieces[0].shape[-1]
    length = pieces[0].shape[1] // 2 * pairs
    shape = jax.ShapeDtypeStruct((rows, chans), BF16)
    scratch = [vmem((2, 2 * slabs, length, chans), BF16)]
    return pl.pallas_call(
        functools.partial(place_kernel, slabs, pairs, held),
        out_shape=[shape] * 2,
        in_specs=[pl.BlockSpec(memory_space=pltpu.SMEM)]
        + [pl.BlockSpec(memory_space=pltpu.VMEM)] * len(pieces),
        out_specs=[pl.BlockSpec(memory_space=pl.ANY)] * 2,
        scratch_shapes=[*scratch, pltpu.SemaphoreType.DMA((2, 2 * slabs))],
        compiler_params=pltpu.CompilerParams(vmem_limit_bytes=vmem_bytes(scratch)),
        name="place",
    )(index, *pieces)


def per_device(inputs, pre_first, occupancy, grad_out, w_first, w_second):
    width, ny, zs, chans = inputs.shape
    slabs, bricks = lax.axis_size("slab"), lax.axis_size("brick")
    pairs, nz = bricks // 2, zs * slabs
    cells_all = width * bricks * ny * nz
    scale = 10.0 / cells_all**0.5
    per = -(-27 // (2 * slabs))
    while per * chans % (16 * pairs):
        per += 1
    rows = per * chans // pairs
    slab, brick = lax.axis_index("slab"), lax.axis_index("brick")
    me = lax.rem(brick, 2)
    index = jnp.stack([me, slab * 2 + me, brick // 2, slab]).astype(jnp.int32)

    occ = occupancy[..., None] != 0
    masked = jnp.where(occ, grad_out, jnp.zeros_like(grad_out))
    pre = jnp.where(occ, pre_first, jnp.full_like(pre_first, EMPTY))
    both = jnp.concatenate([masked, pre], axis=0)
    odd = me == 1
    rim = jnp.concatenate(
        [
            jnp.where(odd, masked[width - 2 :], masked[:2]),
            jnp.where(odd, pre[width - 1 :], pre[:1]),
        ],
        axis=0,
    )

    def swap(b):
        return (b + 1) % bricks if b % 2 else (b - 1) % bricks

    own, in_own = over_slabs(both), over_slabs(inputs)
    rim_own = jnp.concatenate(over_slabs(rim, swap), axis=0)

    wide = jax.ShapeDtypeStruct((9 * chans, 3 * chans), BF16)
    wide_second, wide_first = call(
        widen_kernel, index, [w_second, w_first], [wide, wide], [], 0, "kernels_side_by_side"
    )
    wide_second, rim_own, own[-1], in_own[-1] = lax.optimization_barrier(
        (wide_second, rim_own, own[-1], in_own[-1])
    )
    other = [partner(v, 1) for v in own]
    in_other = [partner(v, 1) for v in in_own]
    rim_other = partner(rim_own, 1)

    shares = [
        jax.ShapeDtypeStruct((pairs // 4, 2 * rows, chans), dtype)
        for dtype in (F32, BF16, BF16, BF16)
    ]
    group = 2 * width * ny * nz
    parts = vmem((3, ny * nz, 3 * chans), F32)
    near = jax.ShapeDtypeStruct((width + 2, ny + 2, nz, chans), BF16)
    near, keep, *sent = call(
        functools.partial(group_kernel, slabs, per, scale),
        index,
        [*own, *other, *in_own, *in_other, rim_own, rim_other, wide_second],
        [near, *shares],
        [
            vmem((3, 2 * width + 4, ny + 2, nz, chans), BF16),
            vmem((3, 2 * width + 2, ny + 2, nz, chans), BF16),
            vmem((2 * width + 2, ny, nz, chans), F32),
            vmem((group, chans), BF16),
            parts,
            vmem((per * chans, chans), F32),
        ],
        2 * group * (27 + 2 * per) * chans * chans,
        "group",
    )
    (grad_in,) = call(
        grad_in_kernel,
        index,
        [near, grad_out, wide_first],
        [jax.ShapeDtypeStruct(inputs.shape, BF16)],
        [vmem((3, *near.shape), BF16), parts],
        2 * group * 9 * chans * chans,
        "grad_in",
    )
    pieces, held, grad_in = combine(keep, sent, pairs, slabs, grad_in)
    pieces = [pieces[r, odd] for r in range(slabs) for odd in range(2)]
    pieces += [partner(v, 1) for v in pieces]
    outs = place(slabs, pairs, held, index, pieces, 27 * chans)
    grad_first, grad_second = (out.reshape(27, chans, chans) for out in outs)
    return (grad_in, grad_first, grad_second)


def solution(mesh):
    in_specs = (
        P("brick", None, "slab", None),
        P("brick", None, "slab", None),
        P("brick", None, "slab"),
        P("brick", None, "slab", None),
        P(),
        P(),
    )
    out_specs = (P("brick", None, "slab", None), P(), P())
    return jax.shard_map(
        per_device, mesh=mesh, in_specs=in_specs, out_specs=out_specs, check_vma=False
    )
```

```python
import functools
import math

import jax
import jax.numpy as jnp
from jax import lax
from jax.experimental import pallas as pl
from jax.experimental.pallas import tpu as pltpu
from jax.sharding import PartitionSpec as P

AXES = ("slab", "brick")
F32 = jnp.float32
BF16 = jnp.bfloat16
OFFSETS = [(a, b, c) for a in (-1, 0, 1) for b in (-1, 0, 1) for c in (-1, 0, 1)]
EMPTY = -9984.0


def send(value, slab_from, brick_from):
    slabs, bricks = lax.axis_size("slab"), lax.axis_size("brick")
    pairs = [
        (slab_from(s) * bricks + brick_from(b), s * bricks + b)
        for s in range(slabs)
        for b in range(bricks)
    ]
    return lax.ppermute(value, AXES, pairs)


def same(index):
    return index


def over_slabs(value, brick_from=same):
    slabs = lax.axis_size("slab")
    pieces = []
    for r in range(slabs):
        if r == 0 and brick_from is same:
            pieces.append(value)
        else:
            pieces.append(send(value, lambda s, r=r: (s + r) % slabs, brick_from))
    return pieces


def partner(value, bit):
    return send(value, same, lambda b: b ^ bit)


def shifted(field_ref, a, b, c, start, planes, nz):
    ny = field_ref.shape[2] - 2
    block = field_ref[c + 1, pl.ds(start - a, planes), pl.ds(1 - b, ny), pl.ds(0, nz), :]
    return block.reshape(planes * ny * nz, block.shape[-1])


def put_planes(field_ref, start, planes):
    n, ny, nz, chans = planes.shape
    flat = planes.reshape(n * ny, nz, chans)
    for c in (-1, 0, 1):
        rolled = flat if c == 0 else pltpu.roll(flat, c % nz, 1)
        rolled = rolled.astype(BF16).reshape(n, ny, nz, chans)
        field_ref[c + 1, pl.ds(start, n), pl.ds(1, ny)] = rolled
        field_ref[c + 1, pl.ds(start, n), pl.ds(0, 1)] = rolled[:, ny - 1 :]
        field_ref[c + 1, pl.ds(start, n), pl.ds(ny + 1, 1)] = rolled[:, :1]


def joined(refs, start, count):
    return jnp.concatenate([r[start : start + count].astype(F32) for r in refs], axis=2)


def fill_second(field_ref, own, other, rim_own, rim_other, me):
    width = own[0].shape[0] // 2
    for i in range(width):
        put_planes(field_ref, 2 + width * me + i, joined(own, i, 1))
        put_planes(field_ref, 2 + width * (1 - me) + i, joined(other, i, 1))
    for i in range(2):
        put_planes(field_ref, (2 + 2 * width) * me + i, joined(rim_own, i, 1))
        put_planes(field_ref, (2 + 2 * width) * (1 - me) + i, joined(rim_other, i, 1))


def sigmoid(v):
    return 1.0 / (1.0 + jnp.exp(-v))


def kernel_terms(left_ref, field_ref, start, planes, nz, scratch_ref, index_ref, per, scale):
    chans = left_ref.shape[-1]

    def step(j):
        k = jnp.minimum(index_ref[1] * per + j, 26)
        a, b, c = k // 9 - 1, (k // 3) % 3 - 1, k % 3 - 1
        cols = shifted(field_ref, a, b, c, start, planes, nz)
        term = lax.dot_general(
            left_ref[...], cols, (((0,), (0,)), ((), ())), preferred_element_type=F32
        )
        scratch_ref[pl.ds(pl.multiple_of(j * chans, chans), chans), :] = term * scale

    if left_ref.shape[0] <= 2048:
        for j in range(per):
            step(j)
    else:
        lax.fori_loop(0, per, lambda j, carry: (step(j), carry)[1], 0)


def put_chunks(scratch_ref, keep_ref, sent_refs, me, tensor):
    count, rows = keep_ref.shape[0], keep_ref.shape[1] // 2
    for i in range(count):
        for rest, ref in enumerate((keep_ref, *sent_refs)):
            at = pl.multiple_of((me ^ (4 * i + rest)) * rows, 8)
            chunk = scratch_ref[pl.ds(at, rows), :].astype(ref.dtype)
            ref[i, pl.ds(tensor * rows, rows), :] = chunk


def convolve(ref, start, planes, depth, w_ref, parts_ref, put):
    ny, chans = ref.shape[2] - 2, ref.shape[4]

    def products(at):
        cols = jnp.concatenate(
            [shifted(ref, 0, b, c, at, 1, depth) for _, b, c in OFFSETS[:9]], axis=1
        )
        return jnp.dot(cols, w_ref[...], preferred_element_type=F32)

    def out(i, part):
        total = sum(part(i - 1 - a)[:, (a + 1) * chans : (a + 2) * chans] for a in (-1, 0, 1))
        put(i - 2, total.reshape(1, ny, depth, chans))

    if ny * depth <= 256:
        parts = []
        for i in range(planes + 2):
            parts.append(products(start - 1 + i))
            if i >= 2:
                out(i, parts.__getitem__)
        return

    rows = pl.ds(0, ny * depth)

    def step(i, carry):
        parts_ref[i % 3, rows] = products(start - 1 + i)
        pl.when(i >= 2)(lambda: out(i, lambda j: parts_ref[(j + 3) % 3, rows]))
        return carry

    lax.fori_loop(0, planes + 2, step, 0)


def widen_kernel(*refs):
    half = len(refs) // 2
    for w_ref, wide_ref in zip(refs[1 : half + 1], refs[half + 1 :], strict=True):
        chans = w_ref.shape[1]
        for k in range(27):
            a, bc = divmod(k, 9)
            block = jnp.transpose(w_ref[k].astype(F32)).astype(BF16)
            wide_ref[pl.ds(bc * chans, chans), pl.ds(a * chans, chans)] = block


def grad_in_kernel(index_ref, near_ref, grad_out_ref, w_ref, grad_in_ref, field_ref, parts_ref):
    planes, padded, nz, chans = near_ref.shape
    width, ny, zs, _ = grad_out_ref.shape
    for i in range(planes):
        put_planes(field_ref, i, near_ref[pl.ds(i, 1), pl.ds(1, ny)].astype(F32))

    def put(i, back):
        grad_in_ref[pl.ds(i, 1)] = (grad_out_ref[pl.ds(i, 1)].astype(F32) + back).astype(BF16)

    convolve(field_ref, 1, width, zs, w_ref, parts_ref, put)


def group_kernel(slabs, per, scale, index_ref, *refs):
    own, other, in_own, in_other = (refs[i * slabs : (i + 1) * slabs] for i in range(4))
    refs = refs[2 * slabs :]
    rim_own, rim_other = (
        [ref.at[pl.ds(3 * r, 3)] for r in range(slabs)] for ref in refs[2 * slabs : 2 * slabs + 2]
    )
    w_second_ref, near_ref, keep_ref, *refs = refs[2 * slabs + 2 :]
    *sent_refs, field_ref, first_ref, pre_ref, left_ref, act_ref, parts_ref, scratch_ref = refs
    me, pair = index_ref[0], index_ref[2]
    width, ny, zs, chans = in_own[0].shape
    nz = zs * slabs
    fill_second(field_ref, own, other, rim_own, rim_other, me)

    def pre_of(i):
        return pre_ref[pl.ds(i, 1)]

    def put_pre(refs_of, i, at):
        pre_ref[pl.ds(at, 1)] = joined(refs_of, i, 1)

    for i in range(width):
        put_pre(own, width + i, 1 + width * me + i)
        put_pre(other, width + i, 1 + width * (1 - me) + i)
    put_pre(rim_own, 2, (1 + 2 * width) * me)
    put_pre(rim_other, 2, (1 + 2 * width) * (1 - me))

    def put_first(i, grad_act):
        pre = pre_of(i)
        sig = sigmoid(pre)
        at = pl.multiple_of(i * ny * nz, ny * nz)
        act_ref[pl.ds(at, ny * nz), :] = (pre * sig).astype(BF16).reshape(ny * nz, chans)
        put_planes(first_ref, i, grad_act * (sig * (1.0 + pre * (1.0 - sig))))

    convolve(field_ref, 1, 2 * width + 2, nz, w_second_ref, parts_ref, put_first)
    near_ref[...] = first_ref[1, pl.ds(width * me, width + 2)]

    for i in range(width):
        for refs_of, who in ((in_own, me), (in_other, 1 - me)):
            rows = joined(refs_of, i, 1).astype(BF16).reshape(ny * nz, chans)
            at = pl.multiple_of((who * width + i) * ny * nz, ny * nz)
            left_ref[pl.ds(at, ny * nz), :] = rows
    kernel_terms(left_ref, first_ref, 1, 2 * width, nz, scratch_ref, index_ref, per, scale)
    put_chunks(scratch_ref, keep_ref, sent_refs, pair, 0)

    act_group = act_ref.at[pl.ds(ny * nz, 2 * width * ny * nz)]
    kernel_terms(act_group, field_ref, 2, 2 * width, nz, scratch_ref, index_ref, per, scale)
    put_chunks(scratch_ref, keep_ref, sent_refs, pair, 1)


def vmem(shape, dtype):
    return pltpu.VMEM(shape, dtype)


def vmem_bytes(scratch):
    held = sum(math.prod(v.shape) * v.dtype.itemsize for v in scratch)
    return min((12 << 20) + held * 3 // 2, 62 << 20)


def call(body, index, operands, out_shape, scratch, flops, name):
    def space(shape):
        return pl.BlockSpec(memory_space=pltpu.SMEM if shape.dtype == jnp.int32 else pltpu.VMEM)

    return pl.pallas_call(
        body,
        out_shape=out_shape,
        in_specs=[space(v) for v in (index, *operands)],
        out_specs=[space(v) for v in out_shape],
        scratch_shapes=scratch,
        compiler_params=pltpu.CompilerParams(vmem_limit_bytes=vmem_bytes(scratch)),
        cost_estimate=pl.CostEstimate(flops=flops, bytes_accessed=4 << 20, transcendentals=0),
        name=name,
    )(index, *operands)


def combine(keep, sent, pairs, slabs, beside):
    total = keep + sum(partner(v, 2 * d).astype(F32) for d, v in enumerate(sent, 1))
    held = list(range(0, pairs, 4))
    middle = [1 << i for i in range(2, pairs.bit_length() - 2)]
    for bit in middle:
        keep = jnp.stack([total[i] for i, r in enumerate(held) if not r & bit])
        sent = jnp.stack([total[i] for i, r in enumerate(held) if r & bit])
        total = keep + partner(sent.astype(BF16), 2 * bit).astype(F32)
        held = [r for r in held if not r & bit]
    mine = lax.reduce_precision(total, 8, 7).astype(BF16)
    got = partner(mine, pairs)
    got, beside = lax.optimization_barrier((got, beside))
    array = (mine.astype(F32) + got[::-1].astype(F32)).astype(BF16)
    for bit in [*middle[::-1], 2]:
        array = jnp.concatenate([array, partner(array, 2 * bit)], axis=0)
        held = held + [r ^ bit for r in held]
    pieces = {(0, 0): array}
    for r in range(slabs):
        for odd in range(2):
            if r or odd:
                pieces[r, odd] = send(
                    array,
                    lambda s, r=r: (s + r) % slabs,
                    lambda b, odd=odd: b ^ (2 * odd),
                )
    return pieces, held, beside


def place_kernel(slabs, pairs, held, index_ref, *refs):
    pieces, outs, scratch_ref, sems = refs[:-4], refs[-4:-2], refs[-2], refs[-1]
    me, pair, slab = index_ref[0], index_ref[2], index_ref[3]
    length = scratch_ref.shape[2]
    rows = length // pairs
    copies = []
    for core in range(2):
        for r in range(slabs):
            share = lax.rem(slab + r, slabs) * 2 + (me ^ core)
            for t, out_ref in enumerate(outs):
                slot = core * slabs + r
                for odd in range(2):
                    for i, d in enumerate(held):
                        at = pl.multiple_of((pair ^ d ^ odd) * rows, 16)
                        piece = pieces[2 * slot + odd]
                        scratch_ref[t, slot, pl.ds(at, rows), :] = piece[i, pl.ds(t * rows, rows), :]
                full, part = divmod(out_ref.shape[0], length)
                cases = [(share < full, length)] + ([(share == full, part)] if part else [])
                start = pl.multiple_of(share * length, 16)
                for case, size in cases:
                    copy = pltpu.make_async_copy(
                        scratch_ref.at[t, slot, pl.ds(0, size)],
                        out_ref.at[pl.ds(start, size)],
                        sems.at[t, slot],
                    )
                    copies.append((case, copy))
                    pl.when(case)(copy.start)
    for case, copy in copies:
        pl.when(case)(copy.wait)


def place(slabs, pairs, held, index, pieces, rows):
    chans = pieces[0].shape[-1]
    length = pieces[0].shape[1] // 2 * pairs
    shape = jax.ShapeDtypeStruct((rows, chans), BF16)
    scratch = [vmem((2, 2 * slabs, length, chans), BF16)]
    return pl.pallas_call(
        functools.partial(place_kernel, slabs, pairs, held),
        out_shape=[shape] * 2,
        in_specs=[pl.BlockSpec(memory_space=pltpu.SMEM)]
        + [pl.BlockSpec(memory_space=pltpu.VMEM)] * len(pieces),
        out_specs=[pl.BlockSpec(memory_space=pl.ANY)] * 2,
        scratch_shapes=[*scratch, pltpu.SemaphoreType.DMA((2, 2 * slabs))],
        compiler_params=pltpu.CompilerParams(vmem_limit_bytes=vmem_bytes(scratch)),
        name="place",
    )(index, *pieces)


def per_device(inputs, pre_first, occupancy, grad_out, w_first, w_second):
    width, ny, zs, chans = inputs.shape
    slabs, bricks = lax.axis_size("slab"), lax.axis_size("brick")
    pairs, nz = bricks // 2, zs * slabs
    cells_all = width * bricks * ny * nz
    scale = 10.0 / cells_all**0.5
    per = -(-27 // (2 * slabs))
    while per * chans % (16 * pairs):
        per += 1
    rows = per * chans // pairs
    slab, brick = lax.axis_index("slab"), lax.axis_index("brick")
    me = lax.rem(brick, 2)
    index = jnp.stack([me, slab * 2 + me, brick // 2, slab]).astype(jnp.int32)

    occ = occupancy[..., None] != 0
    masked = jnp.where(occ, grad_out, jnp.zeros_like(grad_out))
    pre = jnp.where(occ, pre_first, jnp.full_like(pre_first, EMPTY))
    both = jnp.concatenate([masked, pre], axis=0)
    odd = me == 1
    rim = jnp.concatenate(
        [
            jnp.where(odd, masked[width - 2 :], masked[:2]),
            jnp.where(odd, pre[width - 1 :], pre[:1]),
        ],
        axis=0,
    )

    def swap(b):
        return (b + 1) % bricks if b % 2 else (b - 1) % bricks

    own, in_own = over_slabs(both), over_slabs(inputs)
    rim_own = jnp.concatenate(over_slabs(rim, swap), axis=0)

    wide = jax.ShapeDtypeStruct((9 * chans, 3 * chans), BF16)
    wide_second, wide_first = call(
        widen_kernel, index, [w_second, w_first], [wide, wide], [], 0, "kernels_side_by_side"
    )
    wide_second, rim_own, own[-1], in_own[-1] = lax.optimization_barrier(
        (wide_second, rim_own, own[-1], in_own[-1])
    )
    other = [partner(v, 1) for v in own]
    in_other = [partner(v, 1) for v in in_own]
    rim_other = partner(rim_own, 1)

    shares = [
        jax.ShapeDtypeStruct((pairs // 4, 2 * rows, chans), dtype)
        for dtype in (F32, BF16, BF16, BF16)
    ]
    group = 2 * width * ny * nz
    parts = vmem((3, ny * nz, 3 * chans), F32)
    near = jax.ShapeDtypeStruct((width + 2, ny + 2, nz, chans), BF16)
    near, keep, *sent = call(
        functools.partial(group_kernel, slabs, per, scale),
        index,
        [*own, *other, *in_own, *in_other, rim_own, rim_other, wide_second],
        [near, *shares],
        [
            vmem((3, 2 * width + 4, ny + 2, nz, chans), BF16),
            vmem((3, 2 * width + 2, ny + 2, nz, chans), BF16),
            vmem((2 * width + 2, ny, nz, chans), F32),
            vmem((group, chans), BF16),
            vmem((group + 2 * ny * nz, chans), BF16),
            parts,
            vmem((per * chans, chans), F32),
        ],
        2 * group * (27 + 2 * per) * chans * chans,
        "group",
    )
    (grad_in,) = call(
        grad_in_kernel,
        index,
        [near, grad_out, wide_first],
        [jax.ShapeDtypeStruct(inputs.shape, BF16)],
        [vmem((3, *near.shape), BF16), parts],
        2 * group * 9 * chans * chans,
        "grad_in",
    )
    pieces, held, grad_in = combine(keep, sent, pairs, slabs, grad_in)
    pieces = [pieces[r, odd] for r in range(slabs) for odd in range(2)]
    pieces += [partner(v, 1) for v in pieces]
    outs = place(slabs, pairs, held, index, pieces, 27 * chans)
    grad_first, grad_second = (out.reshape(27, chans, chans) for out in outs)
    return (grad_in, grad_first, grad_second)


def solution(mesh):
    in_specs = (
        P("brick", None, "slab", None),
        P("brick", None, "slab", None),
        P("brick", None, "slab"),
        P("brick", None, "slab", None),
        P(),
        P(),
    )
    out_specs = (P("brick", None, "slab", None), P(), P())
    return jax.shard_map(
        per_device, mesh=mesh, in_specs=in_specs, out_specs=out_specs, check_vma=False
    )
```
